128 devices in a mesh: seq: 16 (over x, z), tp: 8 (over y, core).
Axes of the slice: x: 4, y: 4, z: 4, core: 2. Of those that a mesh axis runs over, the one named last changes fastest.
Arguments:
- tokens: bfloat16 [8192, 2880], P(('seq', 'tp')), may hold values from -6 to 6
- attn_gain: float32 [2880], replicated, may hold values from 0.1 to 1.9
- moe_gain: float32 [2880], replicated, may hold values from 0.1 to 1.9
- q_weight: bfloat16 [2880, 8, 512], P('seq', 'tp'), may hold values from -0.109375 to 0.109375
- kv_weight: bfloat16 [2880, 8, 128], P('seq', 'tp'), may hold values from -0.109375 to 0.109375
- o_weight: bfloat16 [512, 8, 2880], P('seq', 'tp'), may hold values from -0.75 to 0.75
- sinks: float32 [8, 8], P('tp'), may hold values from 0 to 6
- gate_up: bfloat16 [128, 2880, 2880], P(('seq', 'tp')), may hold values from -0.109375 to 0.109375
- down: bfloat16 [128, 1440, 2880], P(('seq', 'tp')), may hold values from -0.15625 to 0.15625
- expert_ids: int32 [8192, 4], P(('seq', 'tp')), may hold values from 0 to 127, all different within a row; in each aligned block of 64 rows (0 to 63, 64 to 127, ...) at most 4 rows name the same one
- route_weights: float32 [8192, 4], P(('seq', 'tp')), may hold values from 0.05 to 0.6
Outputs:
- attended: bfloat16 [8192, 2880], P(('seq', 'tp'))
- experts_out: bfloat16 [8192, 2880], P(('seq', 'tp'))
The draws below stay inside these ranges and needn't reach their ends.
Inputs may be any that keep to these rules, and one draw needn't show every extreme that they name: `expert_ids`: A row names 4 different experts. Among the rows of one device (aligned blocks of 64 rows) no expert is named by more than 4 rows, and in every draw some block has an expert named by exactly 4 rows.
All inputs are finite; a program needn't handle non-finite values.
Results may differ from the reference program's by a relative error of at most 0.03.
Values may be sent and summed in bfloat16 or wider, within the bound.
No kernel may reach another device: no remote copies, remote signals or barrier semaphores. Data moves between devices by JAX's collectives and lax.ppermute only.
A program may use at most 128 MiB of HBM per device.

```python
import math
import jax
import jax.numpy as jnp
import numpy as np
from jax import lax

D = 2880
KV_HEADS = 8
GROUP = 8
HD = 64
WINDOW = 128
FFE = 1440
TOPK = 4
TOK_DEV = 512
TOKENS = 8192
ROWS_DEV = 64
EXPERTS = 128
CAP = 4
N_SEQ = 16


def block_levels(stream_key, dims, pieces, low, high):
    level, own = 1.0, jax.random.fold_in(stream_key, 6)
    for position, blocks in pieces:
        draws = jnp.exp(jax.random.uniform(jax.random.fold_in(own, position), (blocks,), jnp.float32, low / len(pieces), high / len(pieces)))
        level = level * jnp.repeat(draws, dims[position] // blocks).reshape([-1 if axis == position else 1 for axis in range(len(dims))])
    return level


def routed_block(key, own, number, rows, amount, top, limit, skew):
    order = jax.random.permutation(key, amount)
    packed, common = shares(amount, rows * top, limit, skew, True), shares(amount, rows * top, limit, skew, False)
    places = jnp.arange(amount)

    def named(lengths, offset_by):
        used = int((lengths > 0).sum())
        fixed = max(1, used // 4)
        shifted = fixed + (places - fixed + offset_by * (used - fixed)) % max(1, amount - fixed)
        return jnp.zeros((amount,), jnp.int32).at[order[jnp.where(places < fixed, places, shifted)]].set(jnp.asarray(lengths, jnp.int32))

    lengths = jnp.where(number % 4 == 0, named(packed, number // 4), named(common, number - number // 4 - 1))
    mixed = jax.random.permutation(jax.random.fold_in(own, 3), amount)
    donor, taker = mixed[0:amount // 2 * 2:2], mixed[1:amount // 2 * 2:2]
    margin = jnp.minimum(lengths[donor] - 1, limit - lengths[taker]) // 2
    margin = jnp.where((donor == order[0]) | (taker == order[0]) | (lengths[taker] == 0), 0, jnp.maximum(margin, 0))
    shifted = jax.random.randint(jax.random.fold_in(own, 4), (amount // 2,), 0, 1 << 20) % (margin + 1)
    lengths = lengths.at[donor].add(-shifted).at[taker].add(shifted)
    members = jnp.searchsorted(jnp.cumsum(lengths), jnp.arange(rows * top), side="right").astype(jnp.int32)
    table = members.reshape(top, rows).T
    table = table[jax.random.permutation(jax.random.fold_in(own, 1), rows)]
    offset_by = jax.random.randint(jax.random.fold_in(own, 2), (rows, 1), 0, top)
    return jnp.take_along_axis(table, (jnp.arange(top)[None, :] + offset_by) % top, axis=1)


def shares(count, total, most, slope, full):
    loads = [(1 << 20) // math.isqrt(standing ** slope) + 1 for standing in range(1, count + 1)]
    largest = most if full else min(most, max(-(-total // count), total * loads[0] // sum(loads)))
    least = 1 if total - largest >= count - 1 else 0
    counts, surplus = [largest] + [least] * (count - 1), total - largest - least * (count - 1)
    while surplus > 0:
        candidates = [i for i in range(1, count) if counts[i] < largest] or [i for i in range(1, count) if counts[i] < most]
        whole, left = sum([loads[i] for i in candidates]), surplus
        for i in candidates:
            addition = min(most - counts[i], max(1, left * loads[i] // whole), surplus)
            counts[i] = counts[i] + addition
            surplus = surplus - addition
    return np.array(counts)


def bell_draw(stream_key, extent, spread, reach, pieces=(), kind=jnp.bfloat16):
    result = jax.random.normal(stream_key, extent, jnp.float32) * spread
    if len(pieces) > 0:
        result = block_levels(stream_key, extent, pieces, -0.22, 0.18) * result
    return jnp.clip(result, min=-reach, max=reach).astype(kind)


def setup_inputs(seed: int = 0) -> dict:
    seeds = jax.random.split(jax.random.key(seed), 12)
    tokens = bell_draw(seeds[0], (TOKENS, D), 1.0, 6.0, ((0, 128),))
    attn_gain = jnp.clip(1.0 + 0.18 * jax.random.normal(seeds[1], (D,), jnp.float32), 0.1, 1.9)
    moe_gain = jnp.clip(1.0 + 0.18 * jax.random.normal(seeds[2], (D,), jnp.float32), 0.1, 1.9)
    q_weight = bell_draw(seeds[3], (D, KV_HEADS, GROUP * HD), D ** -0.5, 0.109375, ((0, 16), (1, 8)))
    kv_weight = bell_draw(seeds[4], (D, KV_HEADS, 2 * HD), D ** -0.5, 0.109375, ((0, 16), (1, 8)))
    o_weight = bell_draw(seeds[5], (GROUP * HD, KV_HEADS, D), HD ** -0.5, 0.75, ((0, 16), (1, 8)))
    sinks = jnp.clip(6.0 * jax.random.uniform(seeds[6], (KV_HEADS, GROUP), jnp.float32) ** block_levels(seeds[6], (KV_HEADS, GROUP), ((0, 8),), -0.2, 0.2), 0.0, 6.0)
    gate_up = bell_draw(seeds[7], (EXPERTS, D, 2 * FFE), D ** -0.5, 0.109375, ((0, 128),))
    down = bell_draw(seeds[8], (EXPERTS, FFE, D), FFE ** -0.5, 0.15625, ((0, 128),))
    expert_ids_keys = jax.random.split(jax.random.fold_in(seeds[9], 1), TOKENS // ROWS_DEV)
    expert_ids_turns = jax.random.permutation(jax.random.fold_in(seeds[9], 3), TOKENS // ROWS_DEV)
    expert_ids = jax.vmap(lambda own, number: routed_block(jax.random.fold_in(seeds[9], 2), own, number, ROWS_DEV, EXPERTS, TOPK, CAP, 2))(expert_ids_keys, expert_ids_turns).reshape((TOKENS, TOPK))
    route_weights = jnp.clip(jnp.exp(math.log(0.6) - 2.4849067 * jax.random.uniform(seeds[10], (TOKENS, TOPK), jnp.float32) ** block_levels(seeds[10], (TOKENS, TOPK), ((0, 128),), -0.2, 0.2)), 0.05, 0.6)
    return {"tokens": tokens, "attn_gain": attn_gain, "moe_gain": moe_gain, "q_weight": q_weight, "kv_weight": kv_weight, "o_weight": o_weight, "sinks": sinks, "gate_up": gate_up, "down": down, "expert_ids": expert_ids, "route_weights": route_weights}


ROPE_BASE = 150000.0

def rms_norm(values, gain):
    wide = values.astype(jnp.float32)
    scale = lax.rsqrt(lax.optimization_barrier(jnp.mean(wide * wide, axis=-1, keepdims=True)) + 1e-05)
    return (wide * scale * gain).astype(jnp.bfloat16)

def rotate(values, positions):
    half = values.shape[-1] // 2
    freq = ROPE_BASE ** (-(jnp.arange(half, dtype=jnp.float32) * 2.0) / (2.0 * half))
    angle = positions * freq
    cosine = jnp.cos(angle)
    sine = jnp.sin(angle)
    first = values[..., :half]
    second = values[..., half:]
    return jnp.concatenate([first * cosine - second * sine, second * cosine + first * sine], axis=-1)

def window_attention(query, keys, values, q_pos, k_pos, sinks, window):
    diff = q_pos[:, None] - k_pos[None, :]
    allowed = (diff >= 0) & (diff < window) & (k_pos[None, :] >= 0)
    scale = query.shape[-1] ** (-0.5)
    scores = jnp.einsum('tjgd,sjd->jgts', query.astype(jnp.float32), keys.astype(jnp.float32)) * scale
    expo = jnp.where(allowed[None, None], jnp.exp(scores), 0.0)
    denom = lax.optimization_barrier(jnp.sum(expo, axis=-1, keepdims=True)) + jnp.exp(sinks)[:, :, None, None]
    probs = (expo / denom).astype(jnp.bfloat16)
    out = jnp.einsum('jgts,sjd->tjgd', probs.astype(jnp.float32), values.astype(jnp.float32))
    return out.astype(jnp.bfloat16).reshape(out.shape[0], out.shape[1], -1)

def expert_ffn(rows, gate_up, down):
    width = down.shape[0]
    both = jnp.dot(rows, gate_up, preferred_element_type=jnp.float32)
    gate = both[:, :width]
    upper = both[:, width:]
    act = ((upper + 1.0) * gate * jax.nn.sigmoid(1.702 * gate)).astype(jnp.bfloat16)
    return jnp.dot(act, down, preferred_element_type=jnp.float32).astype(jnp.bfloat16)

def reference(tokens, attn_gain, moe_gain, q_weight, kv_weight, o_weight, sinks, gate_up, down, expert_ids, route_weights):
    normed = rms_norm(tokens, attn_gain)
    query = jnp.einsum('td,dhe->the', normed.astype(jnp.float32), q_weight.astype(jnp.float32))
    keyval = jnp.einsum('td,dhe->the', normed.astype(jnp.float32), kv_weight.astype(jnp.float32))
    positions = jnp.arange(TOKENS, dtype=jnp.int32)
    pos_float = positions.astype(jnp.float32)
    rq = rotate(query.reshape(TOKENS, KV_HEADS, GROUP, HD), pos_float[:, None, None, None]).astype(jnp.bfloat16)
    rk = rotate(keyval[..., :HD], pos_float[:, None, None]).astype(jnp.bfloat16)
    values = keyval[..., HD:].astype(jnp.bfloat16)
    pad_keys = jnp.concatenate([jnp.zeros((WINDOW, KV_HEADS, HD), jnp.bfloat16), rk], axis=0)
    pad_values = jnp.concatenate([jnp.zeros((WINDOW, KV_HEADS, HD), jnp.bfloat16), values], axis=0)

    def one_block(index):
        start = index * TOK_DEV
        block_q = lax.dynamic_slice_in_dim(rq, start, TOK_DEV, 0)
        block_k = lax.dynamic_slice_in_dim(pad_keys, start, TOK_DEV + WINDOW, 0)
        block_v = lax.dynamic_slice_in_dim(pad_values, start, TOK_DEV + WINDOW, 0)
        q_pos = start + jnp.arange(TOK_DEV, dtype=jnp.int32)
        k_pos = start - WINDOW + jnp.arange(TOK_DEV + WINDOW, dtype=jnp.int32)
        return window_attention(block_q, block_k, block_v, q_pos, k_pos, sinks, WINDOW)
    heads_out = lax.map(one_block, jnp.arange(N_SEQ, dtype=jnp.int32)).reshape(TOKENS, KV_HEADS, GROUP * HD)
    mixed = jnp.einsum('tjg,gjd->td', heads_out.astype(jnp.float32), o_weight.astype(jnp.float32))
    attended = (tokens.astype(jnp.float32) + mixed).astype(jnp.bfloat16)
    moe_in = rms_norm(attended, moe_gain)
    blocks = TOKENS // ROWS_DEV
    picks = expert_ids.reshape(blocks, ROWS_DEV * TOPK)
    onehot = (picks[:, :, None] == jnp.arange(EXPERTS, dtype=jnp.int32)[None, None, :]).astype(jnp.int32)
    earlier = jnp.cumsum(onehot, axis=1) - onehot
    rank = lax.optimization_barrier(jnp.sum(earlier * onehot, axis=2))
    block_ids = jnp.arange(blocks, dtype=jnp.int32)[:, None]
    flat = (picks * (blocks * CAP) + block_ids * CAP + rank).reshape(-1)
    row_of = jnp.arange(TOKENS * TOPK, dtype=jnp.int32) // TOPK
    table_rows = jnp.zeros((EXPERTS * blocks * CAP,), jnp.int32).at[flat].set(row_of)
    table_w = jnp.zeros((EXPERTS * blocks * CAP,), jnp.float32).at[flat].set(route_weights.reshape(-1))
    table_rows = table_rows.reshape(EXPERTS, blocks * CAP)
    table_w = table_w.reshape(EXPERTS, blocks * CAP)

    def step(total, items):
        weight_gu, weight_down, rows, scales = items
        out = expert_ffn(moe_in[rows], weight_gu, weight_down)
        return (total.at[rows].add(scales[:, None] * out.astype(jnp.float32)), None)
    total = lax.scan(step, jnp.zeros((TOKENS, D), jnp.float32), (gate_up, down, table_rows, table_w))[0]
    return (attended, total.astype(jnp.bfloat16))
```

```python
import functools

import jax
import jax.numpy as jnp
from jax import lax
from jax.experimental import pallas as pl
from jax.experimental.pallas import tpu as pltpu
from jax.sharding import Mesh
from jax.sharding import PartitionSpec as P

WINDOW = 128
ROPE_BASE = 150000.0
BF = jnp.bfloat16
F32 = jnp.float32
LOG2E = 1.4426950408889634
OFFSETS = (0, -1, 1, 2)
VMEM = pl.BlockSpec(memory_space=pltpu.VMEM)
SMEM = pl.BlockSpec(memory_space=pltpu.SMEM)
ANY = pl.BlockSpec(memory_space=pl.ANY)


def shifted(block, axis, distance):
    return lax.ppermute(block, axis, [(i, (i + distance) % 4) for i in range(4)])


def swapped(block):
    return lax.ppermute(block, "c", [(0, 1), (1, 0)])


def near(block, axis):
    return shifted(block, axis, 1), shifted(block, axis, -1)


def far(pair, axis, half):
    return shifted(pair[0][:half], axis, 1), shifted(pair[1][half:], axis, -1)


def rms_norm(values, gain):
    wide = values.astype(F32)
    scale = lax.rsqrt(jnp.mean(wide * wide, axis=-1, keepdims=True) + 1e-05)
    return (wide * scale * gain).astype(BF)


def params(limit):
    return pltpu.CompilerParams(vmem_limit_bytes=limit << 20)


def cost(flops, moved):
    return pl.CostEstimate(flops=flops, bytes_accessed=moved, transcendentals=0)


def shard_of(at_ref, first, second, first_is_x):
    dx, dz = (first, second) if first_is_x else (second, first)
    x = lax.rem(at_ref[0] + (OFFSETS[dx] + 4), 4)
    z = lax.rem(at_ref[1] + (OFFSETS[dz] + 4), 4)
    return x * 4 + z


def parts_of(refs):
    own, fore, back, far_a, far_b = refs
    for first in range(4):
        yield first, 0, own, first
        yield first, 1, fore, first
        yield first, 2, back, first
        yield first, 3, (far_a if first < 2 else far_b), first % 2


def rotated(values, cos, sin):
    lanes = values.shape[1]
    lane = lax.broadcasted_iota(jnp.int32, values.shape, 1)
    low = lax.rem(lane, 64) < 32
    other = jnp.where(low, pltpu.roll(values, lanes - 32, 1), pltpu.roll(values, 32, 1))
    return values * cos + other * sin


def row_starts(at_ref):
    for core in range(2):
        for offset in OFFSETS:
            y = lax.rem(at_ref[2] + (offset + 4), 4)
            c = at_ref[3] if core == 0 else 1 - at_ref[3]
            yield pl.multiple_of((y * 2 + c) * 64, 64)


def in_order(at_ref, ref):
    return jnp.concatenate([ref[pl.ds(start, 64), :] for start in row_starts(at_ref)], 0)


def fetched(pairs, sems):
    copies = [pltpu.make_async_copy(a, b, sems.at[i]) for i, (a, b) in enumerate(pairs)]
    for copy in copies:
        copy.start()
    for copy in copies:
        copy.wait()


def token_pairs(xo_ref, xs_ref, x_ref):
    for core, ref in enumerate((xo_ref, xs_ref)):
        for i in range(4):
            start = core * 256 + i * 64
            yield ref.at[i], x_ref.at[start : start + 64]


def weight_pairs(at_ref, refs, first_is_x, columns, w_ref):
    for first, second, ref, index in parts_of(refs):
        shard = shard_of(at_ref, first, second, first_is_x)
        yield ref.at[index, :, columns], w_ref.at[shard]


def projected(x_ref, w_ref):
    rows = x_ref.shape[1] // 16
    total = jnp.zeros((x_ref.shape[0], w_ref.shape[2]), F32)
    for s in range(16):
        x = x_ref[:, s * rows : (s + 1) * rows]
        total += jnp.dot(x, w_ref[s, :rows], preferred_element_type=F32)
    return total


def kv_kernel(at_ref, cos_ref, sin_ref, xo_ref, xs_ref, *refs):
    b_refs, (out_ref, x_ref, w_ref, sems) = refs[:5], refs[5:]
    pairs = list(token_pairs(xo_ref, xs_ref, x_ref))
    pairs += list(weight_pairs(at_ref, b_refs, False, slice(256, 384), w_ref))
    fetched(pairs, sems)
    total = projected(x_ref, w_ref)
    lane = lax.broadcasted_iota(jnp.int32, total.shape, 1)
    turned = rotated(total, in_order(at_ref, cos_ref), in_order(at_ref, sin_ref))
    result = jnp.where(lane < 64, turned, total).astype(BF)
    for i, start in enumerate(row_starts(at_ref)):
        out_ref[pl.ds(start, 64), :] = result[i * 64 : i * 64 + 64]


def q_kernel(at_ref, cos_ref, sin_ref, xo_ref, xs_ref, *refs):
    a_refs, b_refs, (out_ref, x_ref, wa_ref, wb_ref, sems) = refs[:5], refs[5:10], refs[10:]
    pairs = list(token_pairs(xo_ref, xs_ref, x_ref))
    pairs += list(weight_pairs(at_ref, a_refs, True, slice(0, 256), wa_ref))
    pairs += list(weight_pairs(at_ref, b_refs, False, slice(0, 256), wb_ref))
    fetched(pairs, sems)
    cos = jnp.concatenate([in_order(at_ref, cos_ref)] * 2, axis=1)
    sin = jnp.concatenate([in_order(at_ref, sin_ref)] * 2, axis=1)
    for half, w_ref in enumerate((wa_ref, wb_ref)):
        result = rotated(projected(x_ref, w_ref), cos, sin).astype(BF)
        for i, start in enumerate(row_starts(at_ref)):
            out_ref[pl.ds(start, 64), half * 256 : half * 256 + 256] = result[i * 64 : i * 64 + 64]


def attention_kernel(at_ref, q_ref, kv_ref, before_ref, sinks_ref, out_ref, all_ref):
    span = q_ref.shape[0]
    all_ref[:WINDOW] = before_ref[...]
    all_ref[WINDOW:] = kv_ref[...]
    shape = (4 * WINDOW, 2 * WINDOW)
    row = lax.rem(lax.broadcasted_iota(jnp.int32, shape, 0), WINDOW)
    column = lax.broadcasted_iota(jnp.int32, shape, 1)
    inside = (column > row) & (column <= row + WINDOW)
    is_first = (at_ref[0] == 0) & (at_ref[1] == 0)
    pair = lax.broadcasted_iota(jnp.int32, (4 * WINDOW, 1), 0) // WINDOW
    sink = []
    for odd in range(2):
        level = jnp.zeros((4 * WINDOW, 1), F32)
        for p in range(4):
            level = jnp.where(pair == p, sinks_ref[0, 2 * p + odd], level)
        sink.append(jnp.exp2(level * LOG2E - 20.0))
    for i in range(span // WINDOW):
        both = all_ref[i * WINDOW : (i + 2) * WINDOW]
        zero = jnp.zeros((2 * WINDOW, 64), BF)
        key, value = both[:, :64], both[:, 64:]
        keys = jnp.concatenate(
            [jnp.concatenate([key, zero], 1), jnp.concatenate([zero, key], 1)], 0
        )
        values = jnp.concatenate(
            [jnp.concatenate([value, zero], 1), jnp.concatenate([zero, value], 1)], 0
        )
        query = jnp.concatenate(
            [q_ref[i * WINDOW : (i + 1) * WINDOW, p * 128 : (p + 1) * 128] for p in range(4)], 0
        )
        scores = lax.dot_general(
            query, keys, (((1,), (1,)), ((), ())), preferred_element_type=F32
        )
        allowed = inside
        if i == 0:
            allowed = inside & ((column >= WINDOW) | jnp.logical_not(is_first))
        probs = []
        for odd in range(2):
            part = scores[:, odd * 256 : odd * 256 + 256]
            expo = jnp.where(allowed, jnp.exp2(part * (0.125 * LOG2E) - 20.0), 0.0)
            denom = jnp.sum(expo, axis=1, keepdims=True) + sink[odd]
            probs.append((expo * (1.0 / denom)).astype(BF))
        out = jnp.dot(jnp.concatenate(probs, 1), values, preferred_element_type=F32).astype(BF)
        for p in range(4):
            out_ref[i * WINDOW : (i + 1) * WINDOW, p * 128 : (p + 1) * 128] = out[
                p * WINDOW : (p + 1) * WINDOW
            ]


def head_rows(at_ref, heads_ref, is_other):
    c = 1 - at_ref[3] if is_other else at_ref[3]
    rows = []
    for step in range(4):
        start = (lax.rem(at_ref[2] + step, 4) * 2 + c) * 64
        rows.append(heads_ref[pl.ds(pl.multiple_of(start, 64), 64), :])
    return jnp.concatenate(rows, 0)


def other_kernel(at_ref, heads_ref, w_ref, out_ref):
    rows = head_rows(at_ref, heads_ref, True)
    total = jnp.dot(rows, w_ref[...], preferred_element_type=F32).astype(BF)
    for i in range(4):
        out_ref[i] = total[i * 64 : i * 64 + 64]


def own_kernel(at_ref, heads_ref, w_ref, got_ref, up_ref, down_ref, one_ref, three_ref, zero_ref):
    rows = head_rows(at_ref, heads_ref, False)
    total = jnp.dot(rows, w_ref[...], preferred_element_type=F32)
    block = lambda i: total[i * 64 : i * 64 + 64] + got_ref[i].astype(F32)
    far_block = block(2).astype(BF)
    up_ref[...] = far_block[:32]
    down_ref[...] = far_block[32:]
    one_ref[...] = block(1)
    three_ref[...] = block(3)
    zero_ref[...] = block(0)


def dispatch_kernel(place_ref, own_ref, other_ref, out_ref):
    rows = jnp.concatenate([own_ref[...], other_ref[...]], 0)
    out_ref[...] = jnp.dot(place_ref[...], rows, preferred_element_type=F32).astype(BF)


def combine_kernel(weights_ref, rows_ref, own_ref, other_ref):
    both = jnp.dot(weights_ref[...], rows_ref[...], preferred_element_type=F32)
    total = both[:128] + both[128:]
    own_ref[...] = total[:64]
    other_ref[...] = total[64:]


TILE = 512


def activate(both_ref, act_ref, first, last, width):
    for start in range(0, both_ref.shape[0], 64):
        rows = slice(start, start + 64)
        gate = both_ref[rows, first:last]
        upper = both_ref[rows, width + first : width + last]
        act_ref[rows, first:last] = ((upper + 1.0) * gate * jax.nn.sigmoid(1.702 * gate)).astype(BF)


def expert_kernel(steps, width, rows_ref, gu_ref, down_ref, out_ref, both_ref, act_ref):
    step = pl.program_id(0)
    ready = {}
    for first in range(0, width, TILE):
        last = min(first + TILE, width)
        ready.setdefault((width + last - 1) // TILE + 1, []).append((first, last))

    for i in range(steps):

        @pl.when(step == i)
        def _():
            both_ref[:, i * TILE : (i + 1) * TILE] = jnp.dot(
                rows_ref[...], gu_ref[0], preferred_element_type=F32
            )
            for first, last in ready.get(i, ()):
                activate(both_ref, act_ref, first, last, width)

    @pl.when(step == steps)
    def _():
        for first, last in ready.get(steps, ()):
            activate(both_ref, act_ref, first, last, width)

    @pl.when(step >= steps)
    def _():
        out_ref[...] = jnp.dot(act_ref[...], down_ref[0], preferred_element_type=F32).astype(BF)


def expert_ffn(rows, gate_up, down):
    count, model = rows.shape
    width = down.shape[1]
    steps = pl.cdiv(2 * width, TILE)
    return pl.pallas_call(
        functools.partial(expert_kernel, steps, width),
        grid=(steps + pl.cdiv(model, TILE),),
        out_shape=jax.ShapeDtypeStruct((count, model), BF),
        in_specs=[
            pl.BlockSpec((count, model), lambda i: (0, 0)),
            pl.BlockSpec((1, model, TILE), lambda i: (0, 0, jnp.minimum(i, steps - 1))),
            pl.BlockSpec((1, width, TILE), lambda i: (0, 0, jnp.maximum(i - steps, 0))),
        ],
        out_specs=pl.BlockSpec((count, TILE), lambda i: (0, jnp.maximum(i - steps, 0))),
        scratch_shapes=[
            pltpu.VMEM((count, steps * TILE), F32),
            pltpu.VMEM((count, width), BF),
        ],
        compiler_params=params(56),
        cost_estimate=cost(2 * count * model * 3 * width, 31_000_000),
        name="experts",
    )(rows, gate_up, down)


def routing(ids, weights, core, slots, experts):
    count = ids.shape[1]
    total = experts // 2 * 2 * slots
    slot = jnp.arange(total, dtype=jnp.int32)[:, None]
    expert = slot // (2 * slots) * 2 + core
    token = jnp.arange(count, dtype=jnp.int32)
    named = jnp.zeros((total, count), F32)
    weight = jnp.zeros((total, count), F32)
    for j in range(ids.shape[0]):
        same = ids[j][None, :] == expert
        named = named + same.astype(F32)
        weight = weight + jnp.where(same, weights[j][None, :], 0.0)
    half = count // 2
    earlier = (token[:, None] < token[None, :]) & (token[:, None] // half == token[None, :] // half)
    rank = jnp.dot(named.astype(BF), earlier.astype(BF), preferred_element_type=F32)
    here = (rank == (slot % slots).astype(F32)) & (slot // slots % 2 == token[None, :] // half)
    place = jnp.where(here, named, 0.0).astype(BF)
    weighted = jnp.where(here, weight, 0.0).T
    high = lax.reduce_precision(weighted, 8, 7)
    return place, jnp.concatenate([high, weighted - high], 0).astype(BF)


def on_device(
    tokens, attn_gain, moe_gain, q_weight, kv_weight, o_weight, sinks, gate_up, down, expert_ids, route_weights
):
    rows, width = tokens.shape
    barrier = lax.optimization_barrier
    at = jnp.stack([lax.axis_index(a) for a in ("x", "z", "y", "c")]).astype(jnp.int32)

    normed = rms_norm(tokens, attn_gain)
    o_all = lax.all_gather(o_weight[:, 0, :], ("x", "z"), axis=0, tiled=True)
    span = 8 * rows

    q2, kv2 = q_weight[:, 0, :], kv_weight[:, 0, :]
    padded = lambda array: jnp.pad(array, ((0, 4), (0, 0)))
    qa, qb = padded(q2[:, :256]), padded(jnp.concatenate([q2[:, 256:], kv2], axis=1))
    stack = lambda own, pair, rest: jnp.stack([own, *pair, jnp.concatenate(rest)])
    na, nb = near(qa, "x"), near(qb, "z")
    fa, fb = far(na, "x", 96), far(nb, "z", 96)
    sa, sb = stack(qa, na, fa), stack(qb, nb, fb)
    na, nb = near(sa, "z"), near(sb, "x")
    x_parts = (normed, *near(normed, "y"), shifted(normed, "y", 2))
    x_parts = barrier((*x_parts, *na, *nb))[:4]
    x_own = jnp.stack(x_parts)
    x_other = swapped(x_own)
    fa, fb = far(na, "z", 2), far(nb, "x", 2)
    a_parts, b_parts = (sa, *na, *fa), (sb, *nb, *fb)

    half = 32
    freq = ROPE_BASE ** (-(jnp.arange(half, dtype=F32) * 2.0) / (2.0 * half))
    first = (at[0] * 4 + at[1]) * span
    angle = (first + jnp.arange(span, dtype=jnp.int32)).astype(F32)[:, None] * freq
    cos, sin = jnp.cos(angle), jnp.sin(angle)
    cos = jnp.concatenate([cos] * 4, axis=1)
    sin = jnp.concatenate([-sin, sin, -sin, sin], axis=1)

    mine = jnp.concatenate([expert_ids.astype(F32), route_weights], axis=1)
    theirs = swapped(mine)
    table = jnp.concatenate([mine, theirs], axis=0).T
    topk = expert_ids.shape[1]
    place, weighted = routing(table[:topk].astype(jnp.int32), table[topk:], at[3], 4, 128)
    at, place, weighted = barrier((at, place, weighted))

    shard = qa.shape[0]
    x_scratch = pltpu.VMEM((span, width), BF)
    kv = pl.pallas_call(
        kv_kernel,
        out_shape=jax.ShapeDtypeStruct((span, 128), BF),
        in_specs=[SMEM] + [VMEM] * 2 + [ANY] * 7,
        out_specs=VMEM,
        scratch_shapes=[x_scratch, pltpu.VMEM((16, shard, 128), BF), pltpu.SemaphoreType.DMA((24,))],
        compiler_params=params(16),
        cost_estimate=cost(2 * span * width * 128, 8_000_000),
        name="keyval",
    )(at, cos, sin, x_own, x_other, *b_parts)
    before = lax.ppermute(kv[span - WINDOW :], ("x", "z"), [(i, i + 1) for i in range(15)])
    query = pl.pallas_call(
        q_kernel,
        out_shape=jax.ShapeDtypeStruct((span, 512), BF),
        in_specs=[SMEM] + [VMEM] * 2 + [ANY] * 12,
        out_specs=VMEM,
        scratch_shapes=[x_scratch]
        + [pltpu.VMEM((16, shard, 256), BF)] * 2
        + [pltpu.SemaphoreType.DMA((40,))],
        compiler_params=params(20),
        cost_estimate=cost(2 * span * width * 512, 8_000_000),
        name="query",
    )(at, cos, sin, x_own, x_other, *a_parts, *b_parts)
    heads = pl.pallas_call(
        attention_kernel,
        out_shape=jax.ShapeDtypeStruct((span, 512), BF),
        in_specs=[SMEM] + [VMEM] * 3 + [SMEM],
        out_specs=VMEM,
        scratch_shapes=[pltpu.VMEM((span + WINDOW, 128), BF)],
        compiler_params=params(12),
        cost_estimate=cost(4_000_000_000, 2_000_000),
        name="attention",
    )(at, query, kv, before, sinks)
    tile = 768
    steps = pl.cdiv(width, tile)
    columns = lambda count: pl.BlockSpec((count, tile), lambda i: (0, i))
    blocks = pl.BlockSpec((4, rows, tile), lambda i: (0, 0, i))
    common = [SMEM, pl.BlockSpec((span, 512), lambda i: (0, 0)), columns(512)]
    shape = lambda dtype, *dims: jax.ShapeDtypeStruct((*dims, width), dtype)
    other = pl.pallas_call(
        other_kernel,
        grid=(steps,),
        out_shape=shape(BF, 4, rows),
        in_specs=common,
        out_specs=blocks,
        compiler_params=params(16),
        cost_estimate=cost(span * width * 512, 5_000_000),
        name="other",
    )(at, heads, o_all)
    up, down_, one, three, zero = pl.pallas_call(
        own_kernel,
        grid=(steps,),
        out_shape=[shape(BF, 32)] * 2 + [shape(F32, rows)] * 3,
        in_specs=common + [blocks],
        out_specs=[columns(32)] * 2 + [columns(rows)] * 3,
        compiler_params=params(16),
        cost_estimate=cost(span * width * 512, 8_000_000),
        name="own",
    )(at, heads, o_all, swapped(other))
    wide = lambda array: array.astype(F32)
    up, down_ = shifted(up, "y", 1), shifted(down_, "y", -1)
    ahead = jnp.concatenate([one[:32] + wide(up), one[32:]]).astype(BF)
    behind = jnp.concatenate([three[:32], three[32:] + wide(down_)]).astype(BF)
    left, right = shifted(ahead, "y", 1), shifted(behind, "y", -1)
    attended = (wide(tokens) + (zero + wide(left) + wide(right))).astype(BF)
    moe_in = rms_norm(attended, moe_gain)

    slots = place.shape[0]
    outgoing = pl.pallas_call(
        dispatch_kernel,
        out_shape=jax.ShapeDtypeStruct((slots, width), BF),
        in_specs=[VMEM] * 3,
        out_specs=VMEM,
        compiler_params=params(12),
        name="dispatch",
    )(place, moe_in, swapped(moe_in))
    exchange = lambda array: lax.all_to_all(
        array.reshape(64, 8, width), ("x", "z", "y"), split_axis=0, concat_axis=0, tiled=True
    ).reshape(slots, width)
    result = expert_ffn(exchange(outgoing), gate_up, down)
    mine_out, their_out = pl.pallas_call(
        combine_kernel,
        out_shape=[jax.ShapeDtypeStruct((rows, width), F32)] * 2,
        in_specs=[VMEM] * 2,
        out_specs=[VMEM] * 2,
        compiler_params=params(12),
        name="combine",
    )(weighted, exchange(result))
    return attended, (mine_out + swapped(their_out)).astype(BF)


def solution(mesh):
    fine = Mesh(mesh.devices.reshape(4, 4, 4, 2), ("x", "z", "y", "c"))
    seq, tp, every = ("x", "z"), ("y", "c"), ("x", "z", "y", "c")
    placed = (
        P(every, None),
        P(),
        P(),
        P(seq, tp, None),
        P(seq, tp, None),
        P(seq, tp, None),
        P(tp, None),
        P(every, None, None),
        P(every, None, None),
        P(every, None),
        P(every, None),
    )
    return jax.shard_map(
        on_device,
        mesh=fine,
        in_specs=placed,
        out_specs=(P(every, None), P(every, None)),
        check_vma=False,
    )
```

```python
import functools

import jax
import jax.numpy as jnp
from jax import lax
from jax.experimental import pallas as pl
from jax.experimental.pallas import tpu as pltpu
from jax.sharding import Mesh
from jax.sharding import PartitionSpec as P

WINDOW = 128
ROPE_BASE = 150000.0
BF = jnp.bfloat16
F32 = jnp.float32
LOG2E = 1.4426950408889634
OFFSETS = (0, -1, 1, 2)
VMEM = pl.BlockSpec(memory_space=pltpu.VMEM)
SMEM = pl.BlockSpec(memory_space=pltpu.SMEM)


def shifted(block, axis, distance):
    return lax.ppermute(block, axis, [(i, (i + distance) % 4) for i in range(4)])


def swapped(block):
    return lax.ppermute(block, "c", [(0, 1), (1, 0)])


def after(value, *others):
    return lax.optimization_barrier((value, *others))[0]


def near(block, axis):
    return shifted(block, axis, 1), shifted(block, axis, -1)


def passed_on(pair, axis):
    return shifted(pair[0][:2], axis, 1), shifted(pair[1][2:], axis, -1)


def rms_norm(values, gain):
    wide = values.astype(F32)
    scale = lax.rsqrt(jnp.mean(wide * wide, axis=-1, keepdims=True) + 1e-05)
    return (wide * scale * gain).astype(BF)


def params(limit):
    return pltpu.CompilerParams(vmem_limit_bytes=limit << 20)


def cost(flops, moved):
    return pl.CostEstimate(flops=flops, bytes_accessed=moved, transcendentals=0)


def shard_of(at_ref, first, second, first_is_x):
    dx, dz = (first, second) if first_is_x else (second, first)
    x = lax.rem(at_ref[0] + (OFFSETS[dx] + 4), 4)
    z = lax.rem(at_ref[1] + (OFFSETS[dz] + 4), 4)
    return x * 4 + z


def rotated(values, cos, sin):
    lanes = values.shape[1]
    lane = lax.broadcasted_iota(jnp.int32, values.shape, 1)
    low = lax.rem(lane, 64) < 32
    other = jnp.where(low, pltpu.roll(values, lanes - 32, 1), pltpu.roll(values, 32, 1))
    return values * cos + other * sin


def row_starts(at_ref):
    for core in range(2):
        for offset in OFFSETS:
            y = lax.rem(at_ref[2] + (offset + 4), 4)
            c = at_ref[3] if core == 0 else 1 - at_ref[3]
            yield pl.multiple_of((y * 2 + c) * 64, 64)


def in_order(at_ref, ref):
    return jnp.concatenate([ref[pl.ds(start, 64), :] for start in row_starts(at_ref)], 0)


def projection_kernel(at_ref, cos_ref, sin_ref, xo_ref, xs_ref, *refs):
    a_refs, b_refs, (q_ref, kv_ref, x_ref, w_ref) = refs[:5], refs[5:10], refs[10:]
    depth = a_refs[0].shape[1]
    for half, group in enumerate((a_refs, b_refs)):
        for first in range(4):
            for second in range(4):
                ref, index = (group[first], second) if first < 3 else (group[3 + second // 2], second % 2)
                start = shard_of(at_ref, first, second, half == 1) * (2 * depth) + half * depth
                w_ref[pl.ds(pl.multiple_of(start, depth), depth), :] = ref[index]
    for core, ref in enumerate((xo_ref, xs_ref)):
        for i in range(4):
            x_ref[core * 256 + i * 64 : core * 256 + i * 64 + 64] = ref[i]
    total = jnp.dot(x_ref[...], w_ref[...], preferred_element_type=F32)
    cos, sin = in_order(at_ref, cos_ref), in_order(at_ref, sin_ref)
    lane = lax.broadcasted_iota(jnp.int32, cos.shape, 1)
    for column in range(0, 640, 128):
        part = total[:, column : column + 128]
        turned = rotated(part, cos, sin)
        if column == 512:
            turned = jnp.where(lane < 64, turned, part)
        turned = turned.astype(BF)
        for i, start in enumerate(row_starts(at_ref)):
            rows = turned[i * 64 : i * 64 + 64]
            if column == 512:
                kv_ref[pl.ds(start, 64), :] = rows
            else:
                q_ref[pl.ds(start, 64), column : column + 128] = rows


def attended_heads(query, both, allowed, sinks_ref):
    pair = lax.broadcasted_iota(jnp.int32, (4 * WINDOW, 1), 0) // WINDOW
    zero = jnp.zeros((2 * WINDOW, 64), BF)
    key, value = both[:, :64], both[:, 64:]
    keys = jnp.concatenate([jnp.concatenate([key, zero], 1), jnp.concatenate([zero, key], 1)], 0)
    values = jnp.concatenate(
        [jnp.concatenate([value, zero], 1), jnp.concatenate([zero, value], 1)], 0
    )
    query = jnp.concatenate([query[:, p * 128 : (p + 1) * 128] for p in range(4)], 0)
    scores = lax.dot_general(query, keys, (((1,), (1,)), ((), ())), preferred_element_type=F32)
    probs = []
    for odd in range(2):
        level = jnp.zeros((4 * WINDOW, 1), F32)
        for p in range(4):
            level = jnp.where(pair == p, sinks_ref[0, 2 * p + odd], level)
        part = scores[:, odd * 256 : odd * 256 + 256]
        expo = jnp.where(allowed, jnp.exp2(part * (0.125 * LOG2E) - 20.0), 0.0)
        denom = jnp.sum(expo, axis=1, keepdims=True) + jnp.exp2(level * LOG2E - 20.0)
        probs.append((expo * (1.0 / denom)).astype(BF))
    out = jnp.dot(jnp.concatenate(probs, 1), values, preferred_element_type=F32).astype(BF)
    return jnp.concatenate([out[p * WINDOW : (p + 1) * WINDOW] for p in range(4)], 1)


def window_mask():
    shape = (4 * WINDOW, 2 * WINDOW)
    row = lax.rem(lax.broadcasted_iota(jnp.int32, shape, 0), WINDOW)
    column = lax.broadcasted_iota(jnp.int32, shape, 1)
    return (column > row) & (column <= row + WINDOW), column


def later_kernel(q_ref, kv_ref, sinks_ref, out_ref):
    allowed, _ = window_mask()
    for i in range(1, q_ref.shape[0] // WINDOW):
        rows = slice(i * WINDOW, (i + 1) * WINDOW)
        out_ref[(i - 1) * WINDOW : i * WINDOW] = attended_heads(
            q_ref[rows], kv_ref[(i - 1) * WINDOW : (i + 1) * WINDOW], allowed, sinks_ref
        )


def first_kernel(at_ref, q_ref, kv_ref, before_ref, later_ref, sinks_ref, out_ref):
    allowed, column = window_mask()
    is_first = (at_ref[0] == 0) & (at_ref[1] == 0)
    allowed = allowed & ((column >= WINDOW) | jnp.logical_not(is_first))
    both = jnp.concatenate([before_ref[...], kv_ref[...]], 0)
    out_ref[:WINDOW] = attended_heads(q_ref[...], both, allowed, sinks_ref)
    out_ref[WINDOW:] = later_ref[...]


def head_rows(at_ref, heads_ref, is_other):
    c = 1 - at_ref[3] if is_other else at_ref[3]
    rows = []
    for step in range(4):
        start = (lax.rem(at_ref[2] + step, 4) * 2 + c) * 64
        rows.append(heads_ref[pl.ds(pl.multiple_of(start, 64), 64), :])
    return jnp.concatenate(rows, 0)


def other_kernel(at_ref, heads_ref, w_ref, out_ref):
    rows = head_rows(at_ref, heads_ref, True)
    total = jnp.dot(rows, w_ref[...], preferred_element_type=F32).astype(BF)
    for i in range(4):
        out_ref[i] = total[i * 64 : i * 64 + 64]


def own_kernel(at_ref, heads_ref, w_ref, got_ref, up_ref, down_ref, one_ref, three_ref, zero_ref):
    rows = head_rows(at_ref, heads_ref, False)
    total = jnp.dot(rows, w_ref[...], preferred_element_type=F32)
    block = lambda i: total[i * 64 : i * 64 + 64] + got_ref[i].astype(F32)
    far_block = block(2).astype(BF)
    up_ref[...] = far_block[:32]
    down_ref[...] = far_block[32:]
    one_ref[...] = block(1)
    three_ref[...] = block(3)
    zero_ref[...] = block(0)


def dispatch_kernel(place_ref, own_ref, other_ref, out_ref):
    rows = jnp.concatenate([own_ref[...], other_ref[...]], 0)
    out_ref[...] = jnp.dot(place_ref[...], rows, preferred_element_type=F32).astype(BF)


def combine_kernel(weights_ref, rows_ref, own_ref, other_ref):
    both = jnp.dot(weights_ref[...], rows_ref[...], preferred_element_type=F32)
    total = both[:128] + both[128:]
    own_ref[...] = total[:64]
    other_ref[...] = total[64:].astype(BF)


TILE = 512


def activate(both_ref, act_ref, first, last, width):
    for start in range(0, both_ref.shape[0], 64):
        rows = slice(start, start + 64)
        gate = both_ref[rows, first:last]
        upper = both_ref[rows, width + first : width + last]
        act_ref[rows, first:last] = ((upper + 1.0) * gate * jax.nn.sigmoid(1.702 * gate)).astype(BF)


def expert_kernel(steps, width, rows_ref, gu_ref, down_ref, out_ref, both_ref, act_ref):
    step = pl.program_id(0)
    ready = {}
    for first in range(0, width, TILE):
        last = min(first + TILE, width)
        ready.setdefault((width + last - 1) // TILE + 1, []).append((first, last))

    for i in range(steps):

        @pl.when(step == i)
        def _():
            both_ref[:, i * TILE : (i + 1) * TILE] = jnp.dot(
                rows_ref[...], gu_ref[0], preferred_element_type=F32
            )
            for first, last in ready.get(i, ()):
                activate(both_ref, act_ref, first, last, width)

    @pl.when(step == steps)
    def _():
        for first, last in ready.get(steps, ()):
            activate(both_ref, act_ref, first, last, width)

    @pl.when(step >= steps)
    def _():
        out_ref[...] = jnp.dot(act_ref[...], down_ref[0], preferred_element_type=F32).astype(BF)


def expert_ffn(rows, gate_up, down):
    count, model = rows.shape
    width = down.shape[1]
    steps = pl.cdiv(2 * width, TILE)
    return pl.pallas_call(
        functools.partial(expert_kernel, steps, width),
        grid=(steps + pl.cdiv(model, TILE),),
        out_shape=jax.ShapeDtypeStruct((count, model), BF),
        in_specs=[
            pl.BlockSpec((count, model), lambda i: (0, 0)),
            pl.BlockSpec((1, model, TILE), lambda i: (0, 0, jnp.minimum(i, steps - 1))),
            pl.BlockSpec((1, width, TILE), lambda i: (0, 0, jnp.maximum(i - steps, 0))),
        ],
        out_specs=pl.BlockSpec((count, TILE), lambda i: (0, jnp.maximum(i - steps, 0))),
        scratch_shapes=[
            pltpu.VMEM((count, steps * TILE), F32),
            pltpu.VMEM((count, width), BF),
        ],
        compiler_params=params(56),
        cost_estimate=cost(2 * count * model * 3 * width, 31_000_000),
        name="experts",
    )(rows, gate_up, down)


def routing(ids, weights, core, slots, experts):
    count = ids.shape[1]
    total = experts // 2 * 2 * slots
    slot = jnp.arange(total, dtype=jnp.int32)[:, None]
    expert = slot // (2 * slots) * 2 + core
    token = jnp.arange(count, dtype=jnp.int32)
    named = jnp.zeros((total, count), F32)
    weight = jnp.zeros((total, count), F32)
    for j in range(ids.shape[0]):
        same = ids[j][None, :] == expert
        named = named + same.astype(F32)
        weight = weight + jnp.where(same, weights[j][None, :], 0.0)
    half = count // 2
    earlier = (token[:, None] < token[None, :]) & (token[:, None] // half == token[None, :] // half)
    rank = jnp.dot(named.astype(BF), earlier.astype(BF), preferred_element_type=F32)
    here = (rank == (slot % slots).astype(F32)) & (slot // slots % 2 == token[None, :] // half)
    place = jnp.where(here, named, 0.0).astype(BF)
    weighted = jnp.where(here, weight, 0.0).T
    high = lax.reduce_precision(weighted, 8, 7)
    return place, jnp.concatenate([high, weighted - high], 0).astype(BF)


def on_device(
    tokens, attn_gain, moe_gain, q_weight, kv_weight, o_weight, sinks, gate_up, down, expert_ids, route_weights
):
    rows, width = tokens.shape
    barrier = lax.optimization_barrier
    at = jnp.stack([lax.axis_index(a) for a in ("x", "z", "y", "c")]).astype(jnp.int32)

    normed = rms_norm(tokens, attn_gain)
    o_all = lax.all_gather(o_weight[:, 0, :], ("x", "z"), axis=0, tiled=True)
    span = 8 * rows

    shard, depth = q_weight.shape[0], 96
    joined = jnp.concatenate([q_weight[:, 0, :], kv_weight[:, 0, :]], axis=1)
    joined = jnp.pad(joined, ((0, 2 * depth - shard), (0, 0)))
    a, b = joined[:depth], joined[depth:]
    a_near, b_near = near(a, "x"), near(b, "z")
    spread = jnp.pad(normed.reshape(rows, 16, shard), ((0, 0), (0, 0), (0, 2 * depth - shard)))
    spread = spread.reshape(rows, 32 * depth)
    x_fore = shifted(spread, "y", 1)
    a_far = shifted(after(a, *a_near, *b_near), "x", 2)
    b_far = shifted(after(b, *a_near, *b_near), "z", 2)
    x_back = shifted(after(spread, *a_near, *b_near), "y", -1)
    a_stack, b_stack = jnp.stack((a, *a_near, a_far)), jnp.stack((b, *b_near, b_far))
    a_stack, b_stack, _ = barrier((a_stack, b_stack, x_fore))
    x_far = shifted(after(spread, a_stack, b_stack, x_back), "y", 2)
    a_near, b_near = near(a_stack, "z"), near(b_stack, "x")
    *x_parts, a_fore, a_back, b_fore, b_back = barrier(
        (spread, x_fore, x_back, x_far, *a_near, *b_near)
    )
    a_near, b_near = (a_fore, a_back), (b_fore, b_back)
    x_own = jnp.stack(x_parts)
    x_other = swapped(x_own)
    mine = jnp.concatenate([expert_ids.astype(F32), route_weights], axis=1)
    theirs = swapped(after(mine, a_stack, b_stack))
    a_parts = (a_stack, *a_near, *passed_on(a_near, "z"))
    b_parts = (b_stack, *b_near, *passed_on(b_near, "x"))

    half = 32
    freq = ROPE_BASE ** (-(jnp.arange(half, dtype=F32) * 2.0) / (2.0 * half))
    first = (at[0] * 4 + at[1]) * span
    angle = (first + jnp.arange(span, dtype=jnp.int32)).astype(F32)[:, None] * freq
    cos, sin = jnp.cos(angle), jnp.sin(angle)
    cos = jnp.concatenate([cos] * 4, axis=1)
    sin = jnp.concatenate([-sin, sin, -sin, sin], axis=1)

    table = jnp.concatenate([mine, theirs], axis=0).T
    topk = expert_ids.shape[1]
    place, weighted = routing(table[:topk].astype(jnp.int32), table[topk:], at[3], 4, 128)
    at, place, weighted = barrier((at, place, weighted))

    query, kv = pl.pallas_call(
        projection_kernel,
        out_shape=[jax.ShapeDtypeStruct((span, n), BF) for n in (512, 128)],
        in_specs=[SMEM] + [VMEM] * 14,
        out_specs=[VMEM] * 2,
        scratch_shapes=[
            pltpu.VMEM((span, 32 * depth), BF),
            pltpu.VMEM((32 * depth, 640), BF),
        ],
        compiler_params=params(20),
        cost_estimate=cost(2 * span * width * 640, 12_000_000),
        name="projection",
    )(at, cos, sin, x_own, x_other, *a_parts, *b_parts)
    before = lax.ppermute(kv[span - WINDOW :], ("x", "z"), [(i, i + 1) for i in range(15)])
    later = pl.pallas_call(
        later_kernel,
        out_shape=jax.ShapeDtypeStruct((span - WINDOW, 512), BF),
        in_specs=[VMEM] * 2 + [SMEM],
        out_specs=VMEM,
        compiler_params=params(12),
        cost_estimate=cost(3_000_000_000, 2_000_000),
        name="later",
    )(query, kv, sinks)
    before, o_all = barrier((before, o_all))
    heads = pl.pallas_call(
        first_kernel,
        out_shape=jax.ShapeDtypeStruct((span, 512), BF),
        in_specs=[SMEM] + [VMEM] * 4 + [SMEM],
        out_specs=VMEM,
        compiler_params=params(12),
        cost_estimate=cost(1_000_000_000, 1_000_000),
        name="first",
    )(at, query[:WINDOW], kv[:WINDOW], before, later, sinks)

    shape = lambda dtype, *dims: jax.ShapeDtypeStruct((*dims, width), dtype)
    other = pl.pallas_call(
        other_kernel,
        out_shape=shape(BF, 4, rows),
        in_specs=[SMEM] + [VMEM] * 2,
        out_specs=VMEM,
        compiler_params=params(12),
        cost_estimate=cost(span * width * 512, 5_000_000),
        name="other",
    )(at, heads, o_all)
    up, down_, one, three, zero = pl.pallas_call(
        own_kernel,
        out_shape=[shape(BF, 32)] * 2 + [shape(F32, rows)] * 3,
        in_specs=[SMEM] + [VMEM] * 3,
        out_specs=[VMEM] * 5,
        compiler_params=params(12),
        cost_estimate=cost(span * width * 512, 8_000_000),
        name="own",
    )(at, heads, o_all, swapped(other))
    wide = lambda array: array.astype(F32)
    up, down_ = shifted(up, "y", 1), shifted(down_, "y", -1)
    ahead = jnp.concatenate([one[:32] + wide(up), one[32:]]).astype(BF)
    behind = jnp.concatenate([three[:32], three[32:] + wide(down_)]).astype(BF)
    left, right = shifted(ahead, "y", 1), shifted(behind, "y", -1)
    attended = (wide(tokens) + (zero + wide(left) + wide(right))).astype(BF)
    moe_in = rms_norm(attended, moe_gain)

    slots = place.shape[0]
    outgoing = pl.pallas_call(
        dispatch_kernel,
        out_shape=jax.ShapeDtypeStruct((slots, width), BF),
        in_specs=[VMEM] * 3,
        out_specs=VMEM,
        compiler_params=params(12),
        name="dispatch",
    )(place, moe_in, swapped(moe_in))
    exchange = lambda array: lax.all_to_all(
        array.reshape(64, 8, width), ("x", "z", "y"), split_axis=0, concat_axis=0, tiled=True
    ).reshape(slots, width)
    result = expert_ffn(exchange(outgoing), gate_up, down)
    mine_out, their_out = pl.pallas_call(
        combine_kernel,
        out_shape=[jax.ShapeDtypeStruct((rows, width), dtype) for dtype in (F32, BF)],
        in_specs=[VMEM] * 2,
        out_specs=[VMEM] * 2,
        compiler_params=params(12),
        name="combine",
    )(weighted, exchange(result))
    return attended, (mine_out + wide(swapped(their_out))).astype(BF)


def solution(mesh):
    fine = Mesh(mesh.devices.reshape(4, 4, 4, 2), ("x", "z", "y", "c"))
    seq, tp, every = ("x", "z"), ("y", "c"), ("x", "z", "y", "c")
    placed = (
        P(every, None),
        P(),
        P(),
        P(seq, tp, None),
        P(seq, tp, None),
        P(seq, tp, None),
        P(tp, None),
        P(every, None, None),
        P(every, None, None),
        P(every, None),
        P(every, None),
    )
    return jax.shard_map(
        on_device,
        mesh=fine,
        in_specs=placed,
        out_specs=(P(every, None), P(every, None)),
        check_vma=False,
    )
```

```python
import functools

import jax
import jax.numpy as jnp
from jax import lax
from jax.experimental import pallas as pl
from jax.experimental.pallas import tpu as pltpu
from jax.sharding import Mesh
from jax.sharding import PartitionSpec as P

WINDOW = 128
ROPE_BASE = 150000.0
BF = jnp.bfloat16
F32 = jnp.float32
LOG2E = 1.4426950408889634
OFFSETS = (0, -1, 1, 2)
VMEM = pl.BlockSpec(memory_space=pltpu.VMEM)
SMEM = pl.BlockSpec(memory_space=pltpu.SMEM)


def shifted(block, axis, distance):
    return lax.ppermute(block, axis, [(i, (i + distance) % 4) for i in range(4)])


def swapped(block):
    return lax.ppermute(block, "c", [(0, 1), (1, 0)])


def after(value, *others):
    return lax.optimization_barrier((value, *others))[0]


def near(block, axis):
    return shifted(block, axis, 1), shifted(block, axis, -1)


def passed_on(pair, axis):
    return shifted(pair[0][:2], axis, 1), shifted(pair[1][2:], axis, -1)


def rms_norm(values, gain):
    wide = values.astype(F32)
    scale = lax.rsqrt(jnp.mean(wide * wide, axis=-1, keepdims=True) + 1e-05)
    return (wide * scale * gain).astype(BF)


def params(limit):
    return pltpu.CompilerParams(vmem_limit_bytes=limit << 20)


def cost(flops, moved):
    return pl.CostEstimate(flops=flops, bytes_accessed=moved, transcendentals=0)


def shard_of(at_ref, first, second, first_is_x):
    dx, dz = (first, second) if first_is_x else (second, first)
    x = lax.rem(at_ref[0] + (OFFSETS[dx] + 4), 4)
    z = lax.rem(at_ref[1] + (OFFSETS[dz] + 4), 4)
    return x * 4 + z


def rotated(values, cos, sin):
    lanes = values.shape[1]
    lane = lax.broadcasted_iota(jnp.int32, values.shape, 1)
    low = lax.rem(lane, 64) < 32
    other = jnp.where(low, pltpu.roll(values, lanes - 32, 1), pltpu.roll(values, 32, 1))
    return values * cos + other * sin


def row_starts(at_ref):
    for core in range(2):
        for offset in OFFSETS:
            y = lax.rem(at_ref[2] + (offset + 4), 4)
            c = at_ref[3] if core == 0 else 1 - at_ref[3]
            yield pl.multiple_of((y * 2 + c) * 64, 64)


def in_order(at_ref, ref):
    return jnp.concatenate([ref[pl.ds(start, 64), :] for start in row_starts(at_ref)], 0)


def projection_kernel(at_ref, cos_ref, sin_ref, xo_ref, xs_ref, *refs):
    a_refs, b_refs, (q_ref, kv_ref, x_ref, w_ref) = refs[:5], refs[5:10], refs[10:]
    depth = a_refs[0].shape[1]
    for half, group in enumerate((a_refs, b_refs)):
        for first in range(4):
            for second in range(4):
                ref, index = (group[first], second) if first < 3 else (group[3 + second // 2], second % 2)
                start = shard_of(at_ref, first, second, half == 1) * (2 * depth) + half * depth
                w_ref[pl.ds(pl.multiple_of(start, depth), depth), :] = ref[index]
    for core, ref in enumerate((xo_ref, xs_ref)):
        for i in range(4):
            x_ref[core * 256 + i * 64 : core * 256 + i * 64 + 64] = ref[i]
    total = jnp.dot(x_ref[...], w_ref[...], preferred_element_type=F32)
    cos, sin = in_order(at_ref, cos_ref), in_order(at_ref, sin_ref)
    lane = lax.broadcasted_iota(jnp.int32, cos.shape, 1)
    for column in range(0, 640, 128):
        part = total[:, column : column + 128]
        turned = rotated(part, cos, sin)
        if column == 512:
            turned = jnp.where(lane < 64, turned, part)
        turned = turned.astype(BF)
        for i, start in enumerate(row_starts(at_ref)):
            rows = turned[i * 64 : i * 64 + 64]
            if column == 512:
                kv_ref[pl.ds(start, 64), :] = rows
            else:
                q_ref[pl.ds(start, 64), column : column + 128] = rows


def attended_heads(query, both, allowed, sinks_ref):
    pair = lax.broadcasted_iota(jnp.int32, (4 * WINDOW, 1), 0) // WINDOW
    zero = jnp.zeros((2 * WINDOW, 64), BF)
    key, value = both[:, :64], both[:, 64:]
    keys = jnp.concatenate([jnp.concatenate([key, zero], 1), jnp.concatenate([zero, key], 1)], 0)
    values = jnp.concatenate(
        [jnp.concatenate([value, zero], 1), jnp.concatenate([zero, value], 1)], 0
    )
    query = jnp.concatenate([query[:, p * 128 : (p + 1) * 128] for p in range(4)], 0)
    scores = lax.dot_general(query, keys, (((1,), (1,)), ((), ())), preferred_element_type=F32)
    probs = []
    for odd in range(2):
        level = jnp.zeros((4 * WINDOW, 1), F32)
        for p in range(4):
            level = jnp.where(pair == p, sinks_ref[0, 2 * p + odd], level)
        part = scores[:, odd * 256 : odd * 256 + 256]
        expo = jnp.where(allowed, jnp.exp2(part * (0.125 * LOG2E) - 20.0), 0.0)
        denom = jnp.sum(expo, axis=1, keepdims=True) + jnp.exp2(level * LOG2E - 20.0)
        probs.append((expo * (1.0 / denom)).astype(BF))
    out = jnp.dot(jnp.concatenate(probs, 1), values, preferred_element_type=F32).astype(BF)
    return jnp.concatenate([out[p * WINDOW : (p + 1) * WINDOW] for p in range(4)], 1)


def window_mask():
    shape = (4 * WINDOW, 2 * WINDOW)
    row = lax.rem(lax.broadcasted_iota(jnp.int32, shape, 0), WINDOW)
    column = lax.broadcasted_iota(jnp.int32, shape, 1)
    return (column > row) & (column <= row + WINDOW), column


def later_kernel(q_ref, kv_ref, sinks_ref, out_ref):
    allowed, _ = window_mask()
    for i in range(1, q_ref.shape[0] // WINDOW):
        rows = slice(i * WINDOW, (i + 1) * WINDOW)
        out_ref[(i - 1) * WINDOW : i * WINDOW] = attended_heads(
            q_ref[rows], kv_ref[(i - 1) * WINDOW : (i + 1) * WINDOW], allowed, sinks_ref
        )


def first_kernel(at_ref, q_ref, kv_ref, before_ref, later_ref, sinks_ref, out_ref):
    allowed, column = window_mask()
    is_first = (at_ref[0] == 0) & (at_ref[1] == 0)
    allowed = allowed & ((column >= WINDOW) | jnp.logical_not(is_first))
    both = jnp.concatenate([before_ref[...], kv_ref[...]], 0)
    out_ref[:WINDOW] = attended_heads(q_ref[...], both, allowed, sinks_ref)
    out_ref[WINDOW:] = later_ref[...]


def head_rows(at_ref, heads_ref, is_other):
    c = 1 - at_ref[3] if is_other else at_ref[3]
    rows = []
    for step in range(4):
        start = (lax.rem(at_ref[2] + step, 4) * 2 + c) * 64
        rows.append(heads_ref[pl.ds(pl.multiple_of(start, 64), 64), :])
    return jnp.concatenate(rows, 0)


def other_kernel(at_ref, heads_ref, w_ref, out_ref):
    rows = head_rows(at_ref, heads_ref, True)
    total = jnp.dot(rows, w_ref[...], preferred_element_type=F32).astype(BF)
    for i in range(4):
        out_ref[i] = total[i * 64 : i * 64 + 64]


def own_kernel(at_ref, heads_ref, w_ref, got_ref, up_ref, down_ref, one_ref, three_ref, zero_ref):
    rows = head_rows(at_ref, heads_ref, False)
    total = jnp.dot(rows, w_ref[...], preferred_element_type=F32)
    block = lambda i: total[i * 64 : i * 64 + 64] + got_ref[i].astype(F32)
    far_block = block(2).astype(BF)
    up_ref[...] = far_block[:32]
    down_ref[...] = far_block[32:]
    one_ref[...] = block(1)
    three_ref[...] = block(3)
    zero_ref[...] = block(0)


def dispatch_kernel(place_ref, own_ref, other_ref, out_ref):
    rows = jnp.concatenate([own_ref[...], other_ref[...]], 0)
    out_ref[...] = jnp.dot(place_ref[...], rows, preferred_element_type=F32).astype(BF)


def combine_kernel(weights_ref, rows_ref, own_ref, other_ref):
    both = jnp.dot(weights_ref[...], rows_ref[...], preferred_element_type=F32)
    total = both[:128] + both[128:]
    own_ref[...] = total[:64]
    other_ref[...] = total[64:].astype(BF)


TILE = 512


def activate(both_ref, act_ref, first, last, width):
    for start in range(0, both_ref.shape[0], 64):
        rows = slice(start, start + 64)
        gate = both_ref[rows, first:last]
        upper = both_ref[rows, width + first : width + last]
        act_ref[rows, first:last] = ((upper + 1.0) * gate * jax.nn.sigmoid(1.702 * gate)).astype(BF)


def expert_kernel(steps, width, rows_ref, gu_ref, down_ref, out_ref, both_ref, act_ref):
    step = pl.program_id(0)
    ready = {}
    for first in range(0, width, TILE):
        last = min(first + TILE, width)
        ready.setdefault((width + last - 1) // TILE + 1, []).append((first, last))

    for i in range(steps):

        @pl.when(step == i)
        def _():
            both_ref[:, i * TILE : (i + 1) * TILE] = jnp.dot(
                rows_ref[...], gu_ref[0], preferred_element_type=F32
            )
            for first, last in ready.get(i, ()):
                activate(both_ref, act_ref, first, last, width)

    @pl.when(step == steps)
    def _():
        for first, last in ready.get(steps, ()):
            activate(both_ref, act_ref, first, last, width)

    @pl.when(step >= steps)
    def _():
        out_ref[...] = jnp.dot(act_ref[...], down_ref[0], preferred_element_type=F32).astype(BF)


def expert_ffn(rows, gate_up, down):
    count, model = rows.shape
    width = down.shape[1]
    steps = pl.cdiv(2 * width, TILE)
    return pl.pallas_call(
        functools.partial(expert_kernel, steps, width),
        grid=(steps + pl.cdiv(model, TILE),),
        out_shape=jax.ShapeDtypeStruct((count, model), BF),
        in_specs=[
            pl.BlockSpec((count, model), lambda i: (0, 0)),
            pl.BlockSpec((1, model, TILE), lambda i: (0, 0, jnp.minimum(i, steps - 1))),
            pl.BlockSpec((1, width, TILE), lambda i: (0, 0, jnp.maximum(i - steps, 0))),
        ],
        out_specs=pl.BlockSpec((count, TILE), lambda i: (0, jnp.maximum(i - steps, 0))),
        scratch_shapes=[
            pltpu.VMEM((count, steps * TILE), F32),
            pltpu.VMEM((count, width), BF),
        ],
        compiler_params=params(56),
        cost_estimate=cost(2 * count * model * 3 * width, 31_000_000),
        name="experts",
    )(rows, gate_up, down)


def routing(ids, weights, core, slots, experts):
    count = ids.shape[1]
    total = experts // 2 * 2 * slots
    slot = jnp.arange(total, dtype=jnp.int32)[:, None]
    expert = slot // (2 * slots) * 2 + core
    token = jnp.arange(count, dtype=jnp.int32)
    named = jnp.zeros((total, count), F32)
    weight = jnp.zeros((total, count), F32)
    for j in range(ids.shape[0]):
        same = ids[j][None, :] == expert
        named = named + same.astype(F32)
        weight = weight + jnp.where(same, weights[j][None, :], 0.0)
    half = count // 2
    earlier = (token[:, None] < token[None, :]) & (token[:, None] // half == token[None, :] // half)
    rank = jnp.dot(named.astype(BF), earlier.astype(BF), preferred_element_type=F32)
    here = (rank == (slot % slots).astype(F32)) & (slot // slots % 2 == token[None, :] // half)
    place = jnp.where(here, named, 0.0).astype(BF)
    weighted = jnp.where(here, weight, 0.0).T
    high = lax.reduce_precision(weighted, 8, 7)
    return place, jnp.concatenate([high, weighted - high], 0).astype(BF)


def on_device(
    tokens, attn_gain, moe_gain, q_weight, kv_weight, o_weight, sinks, gate_up, down, expert_ids, route_weights
):
    rows, width = tokens.shape
    barrier = lax.optimization_barrier
    at = jnp.stack([lax.axis_index(a) for a in ("x", "z", "y", "c")]).astype(jnp.int32)

    normed = rms_norm(tokens, attn_gain)
    o_all = lax.all_gather(o_weight[:, 0, :], ("x", "z"), axis=0, tiled=True)
    span = 8 * rows

    shard, depth = q_weight.shape[0], 96
    joined = jnp.concatenate([q_weight[:, 0, :], kv_weight[:, 0, :]], axis=1)
    joined = jnp.pad(joined, ((0, 2 * depth - shard), (0, 0)))
    a, b = joined[:depth], joined[depth:]
    a_near, b_near = near(a, "x"), near(b, "z")
    spread = jnp.pad(normed.reshape(rows, 16, shard), ((0, 0), (0, 0), (0, 2 * depth - shard)))
    spread = spread.reshape(rows, 32 * depth)
    mine = jnp.concatenate([expert_ids.astype(F32), route_weights], axis=1)
    theirs = swapped(mine)
    x_fore = shifted(after(spread, theirs), "y", 1)
    a_far = shifted(after(a, *a_near, *b_near), "x", 2)
    b_far = shifted(after(b, *a_near, *b_near), "z", 2)
    x_back = shifted(after(spread, *a_near, *b_near), "y", -1)
    a_stack, b_stack = jnp.stack((a, *a_near, a_far)), jnp.stack((b, *b_near, b_far))
    a_stack, b_stack, _ = barrier((a_stack, b_stack, x_fore))
    x_far = shifted(after(spread, a_stack, b_stack, x_back), "y", 2)
    a_near, b_near = near(a_stack, "z"), near(b_stack, "x")
    *x_parts, a_fore, a_back, b_fore, b_back = barrier(
        (spread, x_fore, x_back, x_far, *a_near, *b_near)
    )
    a_near, b_near = (a_fore, a_back), (b_fore, b_back)
    x_own = jnp.stack(x_parts)
    x_other = swapped(x_own)
    a_parts = (a_stack, *a_near, *passed_on(a_near, "z"))
    b_parts = (b_stack, *b_near, *passed_on(b_near, "x"))

    half = 32
    freq = ROPE_BASE ** (-(jnp.arange(half, dtype=F32) * 2.0) / (2.0 * half))
    first = (at[0] * 4 + at[1]) * span
    angle = (first + jnp.arange(span, dtype=jnp.int32)).astype(F32)[:, None] * freq
    cos, sin = jnp.cos(angle), jnp.sin(angle)
    cos = jnp.concatenate([cos] * 4, axis=1)
    sin = jnp.concatenate([-sin, sin, -sin, sin], axis=1)

    table = jnp.concatenate([mine, theirs], axis=0).T
    topk = expert_ids.shape[1]
    place, weighted = routing(table[:topk].astype(jnp.int32), table[topk:], at[3], 4, 128)
    at, place, weighted = barrier((at, place, weighted))

    query, kv = pl.pallas_call(
        projection_kernel,
        out_shape=[jax.ShapeDtypeStruct((span, n), BF) for n in (512, 128)],
        in_specs=[SMEM] + [VMEM] * 14,
        out_specs=[VMEM] * 2,
        scratch_shapes=[
            pltpu.VMEM((span, 32 * depth), BF),
            pltpu.VMEM((32 * depth, 640), BF),
        ],
        compiler_params=params(20),
        cost_estimate=cost(2 * span * width * 640, 12_000_000),
        name="projection",
    )(at, cos, sin, x_own, x_other, *a_parts, *b_parts)
    before = lax.ppermute(kv[span - WINDOW :], ("x", "z"), [(i, i + 1) for i in range(15)])
    later = pl.pallas_call(
        later_kernel,
        out_shape=jax.ShapeDtypeStruct((span - WINDOW, 512), BF),
        in_specs=[VMEM] * 2 + [SMEM],
        out_specs=VMEM,
        compiler_params=params(12),
        cost_estimate=cost(3_000_000_000, 2_000_000),
        name="later",
    )(query, kv, sinks)
    before, o_all = barrier((before, o_all))
    heads = pl.pallas_call(
        first_kernel,
        out_shape=jax.ShapeDtypeStruct((span, 512), BF),
        in_specs=[SMEM] + [VMEM] * 4 + [SMEM],
        out_specs=VMEM,
        compiler_params=params(12),
        cost_estimate=cost(1_000_000_000, 1_000_000),
        name="first",
    )(at, query[:WINDOW], kv[:WINDOW], before, later, sinks)

    shape = lambda dtype, *dims: jax.ShapeDtypeStruct((*dims, width), dtype)
    other = pl.pallas_call(
        other_kernel,
        out_shape=shape(BF, 4, rows),
        in_specs=[SMEM] + [VMEM] * 2,
        out_specs=VMEM,
        compiler_params=params(12),
        cost_estimate=cost(span * width * 512, 5_000_000),
        name="other",
    )(at, heads, o_all)
    up, down_, one, three, zero = pl.pallas_call(
        own_kernel,
        out_shape=[shape(BF, 32)] * 2 + [shape(F32, rows)] * 3,
        in_specs=[SMEM] + [VMEM] * 3,
        out_specs=[VMEM] * 5,
        compiler_params=params(12),
        cost_estimate=cost(span * width * 512, 8_000_000),
        name="own",
    )(at, heads, o_all, swapped(other))
    wide = lambda array: array.astype(F32)
    up, down_ = shifted(up, "y", 1), shifted(down_, "y", -1)
    ahead = jnp.concatenate([one[:32] + wide(up), one[32:]]).astype(BF)
    behind = jnp.concatenate([three[:32], three[32:] + wide(down_)]).astype(BF)
    left, right = shifted(ahead, "y", 1), shifted(behind, "y", -1)
    attended = (wide(tokens) + (zero + wide(left) + wide(right))).astype(BF)
    moe_in = rms_norm(attended, moe_gain)

    slots = place.shape[0]
    outgoing = pl.pallas_call(
        dispatch_kernel,
        out_shape=jax.ShapeDtypeStruct((slots, width), BF),
        in_specs=[VMEM] * 3,
        out_specs=VMEM,
        compiler_params=params(12),
        name="dispatch",
    )(place, moe_in, swapped(moe_in))
    exchange = lambda array: lax.all_to_all(
        array.reshape(64, 8, width), ("x", "z", "y"), split_axis=0, concat_axis=0, tiled=True
    ).reshape(slots, width)
    result = expert_ffn(exchange(outgoing), gate_up, down)
    mine_out, their_out = pl.pallas_call(
        combine_kernel,
        out_shape=[jax.ShapeDtypeStruct((rows, width), dtype) for dtype in (F32, BF)],
        in_specs=[VMEM] * 2,
        out_specs=[VMEM] * 2,
        compiler_params=params(12),
        name="combine",
    )(weighted, exchange(result))
    return attended, (mine_out + wide(swapped(their_out))).astype(BF)


def solution(mesh):
    fine = Mesh(mesh.devices.reshape(4, 4, 4, 2), ("x", "z", "y", "c"))
    seq, tp, every = ("x", "z"), ("y", "c"), ("x", "z", "y", "c")
    placed = (
        P(every, None),
        P(),
        P(),
        P(seq, tp, None),
        P(seq, tp, None),
        P(seq, tp, None),
        P(tp, None),
        P(every, None, None),
        P(every, None, None),
        P(every, None),
        P(every, None),
    )
    return jax.shard_map(
        on_device,
        mesh=fine,
        in_specs=placed,
        out_specs=(P(every, None), P(every, None)),
        check_vma=False,
    )
```
